32 devices in a mesh: groups: 2 (over y), lat: 4 (over z), slc: 2 (over x), rep: 2 (over core).
Axes of the slice: x: 2, y: 2, z: 4, core: 2. Of those that a mesh axis runs over, the one named last changes fastest.
Arguments:
- atom_xy: float32 [8, 2, 2, 256], P(('groups', 'lat'), 'slc'), parts along dimension 0, may hold values from 0 to 4096, as said below
- atom_species: int32 [8, 2, 256], P(('groups', 'lat'), 'slc'), parts along dimension 0, may hold values from 0 to 7
- atom_slab: int32 [8, 2, 256], P(('groups', 'lat'), 'slc'), parts along dimension 0, may hold values from 0 to 1
- species_amp: float32 [8], replicated, may hold values from 0.5 to 3
- species_spread: float32 [8], replicated, may hold values from 2 to 6
- margin: int32 [8, 2, 2, 2, 3, 128], P(('groups', 'lat'), 'slc', None, 'rep'), parts along dimension 0, may hold values from -1 to 255, as said below
- probe_pos: int32 [64, 2], P(('groups', 'lat', 'slc', 'rep')), parts along dimension 0, may hold values from 0 to 4092, as said below
Outputs:
- exit_wave: bfloat16 [64, 256, 2, 256], P(('groups', 'lat', 'slc', 'rep')), parts along dimension 0
The draws below stay inside these ranges and needn't reach their ends.
There are 2 independent parts, one for each index of `groups`. The reference program is written for one: setup_inputs(seed, part) draws one part's arguments, and reference() takes and returns one part's arrays. A program takes and returns all parts, laid end to end along the dimension named above; an argument that names none is the same for every part. Nothing has to cross between parts.
Inputs may be any that keep to these rules, and one draw needn't show every extreme that they name: `atom_xy`: atom a of tile v has x between (v * 256 + a) b and (v * 256 + a + 1) b with b = 4, and y in [0, 256). `probe_pos`: the 2 probes of one lateral index, slice owner and rep index share their x anchor; the centre of each window lies in tile t, x is a multiple of 4 taken modulo 4096, and y is below 256. `margin`: each block lists a run of consecutive local atom indices in rising order, then -1: the atoms of tile v whose x lies within 128 pixels of the probes' windows (x modulo 4096).
All inputs are finite; a program needn't handle non-finite values.
Results may differ from the reference program's by a relative error of at most 0.03.
Values may be sent and summed in bfloat16 or wider, within the bound.
A program may use at most 128 MiB of HBM per device.

```python
import math
import jax
import jax.numpy as jnp
from jax import lax

W = 256
SL_DEV = 2
PB_DEV = 2
ATOM_DEV = 256
CAP = 128
NSPEC = 8
PROBES = 32
N_LAT = 4
N_SLC = 2
N_REP = 2


def batch_centres(key):
    base_key = jax.random.fold_in(key, 29)
    key_low, key_high, key_any, key_first, key_second = jax.random.split(base_key, 5)
    block_shape = (N_LAT, N_SLC, N_REP)
    low_band = jax.random.randint(key_low, block_shape, 0, CAP // 4)
    lateral_zero = jnp.arange(N_LAT, dtype=jnp.int32)[:, None, None] == 0
    rep_zero = jnp.arange(N_REP, dtype=jnp.int32)[None, None, :] == 0
    low_band = jnp.where(lateral_zero & rep_zero, CAP // 4 - 1, low_band)
    high_band = jax.random.randint(key_high, block_shape, ATOM_DEV - CAP // 4 + 1, ATOM_DEV)
    any_band = jax.random.randint(key_any, block_shape, 0, ATOM_DEV)
    first_slot = jax.random.randint(key_first, (N_LAT, 1, N_REP), 0, N_SLC)
    second_slot = (first_slot + jax.random.randint(key_second, (N_LAT, 1, N_REP), 1, N_SLC)) % N_SLC
    slot_index = jnp.arange(N_SLC, dtype=jnp.int32)[None, :, None]
    picked = jnp.where(slot_index == first_slot, low_band, jnp.where(slot_index == second_slot, high_band, any_band))
    return picked.astype(jnp.int32)


def draw_atom_xy(key, part):
    base_key = jax.random.fold_in(key, 5)
    key_jitter, key_along = jax.random.split(base_key, 2)
    cell_size = 2.0 * W / CAP
    tile_index = jnp.arange(N_LAT, dtype=jnp.float32)[:, None, None]
    atom_index = jnp.arange(ATOM_DEV, dtype=jnp.float32)[None, None, :]
    jitter = jax.random.uniform(key_jitter, (N_LAT, N_SLC, ATOM_DEV), jnp.float32, 0.1, 0.9)
    across_x = (tile_index * ATOM_DEV + atom_index + jitter) * cell_size
    along_y = jax.random.uniform(key_along, (N_LAT, N_SLC, ATOM_DEV), jnp.float32, 0.0, 1.0) * W
    return jnp.stack([across_x, along_y], 2).astype(jnp.float32)


def draw_probe_pos(key, part):
    centres = batch_centres(key)
    cell_size = 2 * W // CAP
    tile_width = ATOM_DEV * cell_size
    field_width = N_LAT * tile_width
    tile_index = jnp.arange(N_LAT, dtype=jnp.int32)[:, None, None]
    anchor_x = (tile_index * tile_width + centres * cell_size - W // 2) % field_width
    anchor_x = jnp.broadcast_to(anchor_x[..., None], (N_LAT, N_SLC, N_REP, PB_DEV)).reshape(-1)
    anchor_y = jax.random.randint(jax.random.fold_in(key, 31), (PROBES,), 0, W)
    return jnp.stack([anchor_x, anchor_y], 1).astype(jnp.int32)


def draw_margin(key, part):
    centres = batch_centres(key)
    tile_index = jnp.arange(N_LAT, dtype=jnp.int32)[:, None]
    offsets = jnp.arange(3, dtype=jnp.int32)[None, :]
    target = (tile_index + offsets - 1) % N_LAT
    seen = jnp.transpose(centres[target], (0, 2, 3, 1))
    relative = seen - CAP // 2 + (jnp.arange(3, dtype=jnp.int32)[None, None, None, :] - 1) * ATOM_DEV
    run_start = jnp.maximum(relative, 0)
    run_end = jnp.minimum(relative + CAP, ATOM_DEV)
    run_length = jnp.maximum(run_end - run_start, 0)
    entries = jnp.arange(CAP, dtype=jnp.int32)
    listed = jnp.where(entries < run_length[..., None], run_start[..., None] + entries, -1)
    listed = jnp.broadcast_to(listed[:, None], (N_LAT, N_SLC, N_SLC, N_REP, 3, CAP))
    return listed.astype(jnp.int32)


def with_ends(drawn, rng, low, high):
    longest = drawn.shape.index(max(drawn.shape))
    spots = []
    for shift in (0, 1):
        where = [jax.random.randint(jax.random.fold_in(rng, axis), (), 0, length) for axis, length in enumerate(drawn.shape)]
        where[longest] = (where[longest] + shift) % drawn.shape[longest]
        spots.append(tuple(where))
    return drawn.at[spots[0]].set(low).at[spots[1]].set(high)


def setup_inputs(seed: int = 0, part: int = 0) -> dict:
    streams_of = jax.random.split(jax.random.key(seed), 8)
    part_keys = jax.random.split(jax.random.fold_in(streams_of[7], part), 8)
    return {
        "atom_xy": draw_atom_xy(jax.random.fold_in(jax.random.fold_in(streams_of[7], part), 71), part),
        "atom_species": with_ends(jax.random.randint(part_keys[1], (N_LAT, N_SLC, ATOM_DEV), 0, NSPEC), jax.random.fold_in(part_keys[1], 1), 0, NSPEC - 1).astype(jnp.int32),
        "atom_slab": with_ends(jax.random.randint(part_keys[2], (N_LAT, N_SLC, ATOM_DEV), 0, SL_DEV), jax.random.fold_in(part_keys[2], 1), 0, SL_DEV - 1).astype(jnp.int32),
        "species_amp": jnp.clip(jnp.exp(jax.random.uniform(streams_of[3], (NSPEC,), jnp.float32, math.log(0.5), math.log(3.0))), 0.5, 3.0),
        "species_spread": jnp.clip(jnp.exp(jax.random.uniform(streams_of[4], (NSPEC,), jnp.float32, math.log(2.0), math.log(6.0))), 2.0, 6.0),
        "margin": draw_margin(jax.random.fold_in(jax.random.fold_in(streams_of[7], part), 71), part),
        "probe_pos": draw_probe_pos(jax.random.fold_in(jax.random.fold_in(streams_of[7], part), 71), part),
    }


PROPAGATION_COEF = 0.001
DEFOCUS_COEF = 4.19

def centered_frequency(window):
    indices = jnp.arange(window, dtype=jnp.int32)
    return jnp.where(indices < window // 2, indices, indices - window).astype(jnp.float32)

def transform_matrices(window, direction):
    indices = jnp.arange(window, dtype=jnp.int32)
    product = indices[:, None] * indices[None, :] % window
    angle_table = 2.0 * math.pi / window * product.astype(jnp.float32)
    real_part = (jnp.cos(angle_table) / math.sqrt(window)).astype(jnp.bfloat16)
    imag_part = (direction * jnp.sin(angle_table) / math.sqrt(window)).astype(jnp.bfloat16)
    right_matrix = jnp.stack([jnp.stack([real_part, imag_part], 0), jnp.stack([-imag_part, real_part], 0)], 0)
    right_matrix = jnp.transpose(right_matrix, (0, 2, 1, 3)).reshape(2 * window, 2 * window)
    left_matrix = jnp.stack([jnp.stack([real_part, -imag_part], -1), jnp.stack([imag_part, real_part], -1)], 1)
    left_matrix = left_matrix.reshape(2 * window, 2 * window)
    return (left_matrix, right_matrix)

def propagator(window):
    frequency = centered_frequency(window)
    radius = frequency[:, None] * frequency[:, None] + frequency[None, :] * frequency[None, :]
    inside = (9.0 * radius < window * window).astype(jnp.float32)
    phase_angle = -PROPAGATION_COEF * (65536.0 / (window * window)) * radius
    return (inside * jnp.cos(phase_angle), inside * jnp.sin(phase_angle))

def left_apply(left_matrix, probe_wave):
    window = probe_wave.shape[0]
    return jnp.dot(left_matrix, probe_wave.reshape(2 * window, window), preferred_element_type=jnp.float32).reshape(window, 2, window)

def right_apply(right_matrix, probe_wave):
    window = probe_wave.shape[0]
    return jnp.dot(probe_wave.reshape(window, 2 * window), right_matrix, preferred_element_type=jnp.float32).reshape(window, 2, window)

def incident(window, inverse_left, inverse_right):
    frequency = centered_frequency(window)
    radius = frequency[:, None] * frequency[:, None] + frequency[None, :] * frequency[None, :]
    inside = (16.0 * radius < window * window).astype(jnp.float32)
    norm_scale = window / jnp.sqrt(jnp.sum(inside))
    phase_angle = -(DEFOCUS_COEF / window) * radius
    spectrum = jnp.stack([inside * norm_scale * jnp.cos(phase_angle), inside * norm_scale * jnp.sin(phase_angle)], 1).astype(jnp.bfloat16)
    start_rows = left_apply(inverse_left, spectrum).astype(jnp.bfloat16)
    return right_apply(inverse_right, start_rows).astype(jnp.bfloat16)

def one_slice(probe_wave, potential, tables):
    forward_left, forward_right, inverse_left, inverse_right, prop_real, prop_imag = tables
    cos_phase = jnp.cos(potential)
    sin_phase = jnp.sin(potential)
    real_part = probe_wave[:, 0, :].astype(jnp.float32)
    imag_part = probe_wave[:, 1, :].astype(jnp.float32)
    transmitted = jnp.stack([real_part * cos_phase - imag_part * sin_phase, real_part * sin_phase + imag_part * cos_phase], 1).astype(jnp.bfloat16)
    rowwise = right_apply(forward_right, transmitted).astype(jnp.bfloat16)
    spectrum = left_apply(forward_left, rowwise)
    spec_real = spectrum[:, 0, :]
    spec_imag = spectrum[:, 1, :]
    spectrum = jnp.stack([spec_real * prop_real - spec_imag * prop_imag, spec_real * prop_imag + spec_imag * prop_real], 1).astype(jnp.bfloat16)
    back_rows = left_apply(inverse_left, spectrum).astype(jnp.bfloat16)
    return right_apply(inverse_right, back_rows).astype(jnp.bfloat16)

def atom_fields(positions, species, slab, species_amp, species_spread, layers):
    species_match = (species[None, :] == jnp.arange(species_amp.shape[0], dtype=jnp.int32)[:, None]).astype(species_amp.dtype)
    amplitude = lax.optimization_barrier(jnp.sum(species_match * species_amp[:, None], 0))
    spread = lax.optimization_barrier(jnp.sum(species_match * species_spread[:, None], 0))
    inverse = 0.5 / (spread * spread)
    slab_match = (slab[None, :] == jnp.arange(layers, dtype=jnp.int32)[:, None]).astype(amplitude.dtype)
    return jnp.concatenate([positions, inverse[None, :], slab_match * amplitude[None, :]], 0)

def pick_rows(fields, pick_list):
    valid_mask = (pick_list >= 0).astype(fields.dtype)
    safe_index = jnp.maximum(pick_list, 0)
    gathered = fields[:, safe_index]
    return jnp.concatenate([gathered[:3], gathered[3:] * valid_mask[None]], 0)

def slab_potential(row_block, anchor, window, layers, field_x):
    pixels = jnp.arange(window, dtype=jnp.float32)
    half_width = 0.5 * window
    half_field = 0.5 * field_x
    inverse = row_block[2][:, None]
    dist_x = jnp.mod(row_block[0][:, None] - anchor[0].astype(jnp.float32) - pixels[None, :] + half_field, field_x) - half_field
    across = jnp.exp(-dist_x * dist_x * inverse).astype(jnp.bfloat16)
    dist_y = jnp.mod(row_block[1][:, None] - anchor[1].astype(jnp.float32) - pixels[None, :] + half_width, window) - half_width
    along = jnp.exp(-dist_y * dist_y * inverse)
    weighted = (row_block[3:3 + layers][:, :, None] * along[None]).astype(jnp.bfloat16)
    weighted = jnp.transpose(weighted, (1, 0, 2)).reshape(row_block.shape[1], layers * window)
    return jnp.dot(across.T, weighted, preferred_element_type=jnp.float32).reshape(window, layers, window)

def reference(atom_xy, atom_species, atom_slab, species_amp, species_spread, margin, probe_pos):
    layers = SL_DEV
    field_x = N_LAT * ATOM_DEV * (2 * W // CAP)
    forward_left, forward_right = transform_matrices(W, -1.0)
    inverse_left, inverse_right = transform_matrices(W, 1.0)
    prop_real, prop_imag = propagator(W)
    tables = (forward_left, forward_right, inverse_left, inverse_right, prop_real, prop_imag)
    start_wave = incident(W, inverse_left, inverse_right)

    def device_fields(positions, species, slab):
        return atom_fields(positions, species, slab, species_amp, species_spread, layers)
    field_table = jax.vmap(jax.vmap(device_fields))(atom_xy, atom_species, atom_slab)

    def run_probe(probe_index):
        lateral = probe_index // (PB_DEV * N_REP * N_SLC)
        entry_slot = probe_index // (PB_DEV * N_REP) % N_SLC
        replica = probe_index // PB_DEV % N_REP
        anchor = probe_pos[probe_index]
        probe_wave = start_wave
        for hop_index in range(N_SLC):
            owner_slot = (entry_slot + hop_index) % N_SLC
            blocks = []
            for offset in (2, 1, 0):
                source = (lateral - offset + 1) % N_LAT
                owner_fields = field_table[source, owner_slot]
                pick_list = margin[source, owner_slot, entry_slot, replica, offset]
                blocks.append(pick_rows(owner_fields, pick_list))
            row_block = jnp.concatenate(blocks, 1)
            potential = slab_potential(row_block, anchor, W, layers, field_x)
            for layer_index in range(layers):
                probe_wave = one_slice(probe_wave, potential[:, layer_index, :], tables)
        return probe_wave
    return lax.map(run_probe, jnp.arange(PROBES, dtype=jnp.int32))
```

```python
import functools
import math

import jax
import jax.numpy as jnp
import ml_dtypes
import numpy as np
from jax import lax
from jax.experimental import pallas as pl
from jax.experimental.pallas import tpu as pltpu
from jax.sharding import PartitionSpec as P

PROPAGATION_COEF = 0.001
DEFOCUS_COEF = 4.19
LOG2E = math.log2(math.e)
MESH = pl.DeviceIdType.MESH

LANES = 128


def real_basis(window):
    top = max(k for k in range(window // 2) if 9 * k * k < window * window)
    freq = np.concatenate([np.arange(top + 1), np.arange(1, top + 1)])
    pixel = np.arange(window)
    angle = 2.0 * np.pi / window * (pixel[:, None] * freq[None, :] % window)
    basis = np.where(np.arange(freq.size) <= top, np.cos(angle), np.sin(angle))
    norm = np.where(freq == 0, 1.0, 2.0) / window
    return basis, freq, norm


@functools.cache
def tables(window):
    basis, freq, norm = real_basis(window)
    count = freq.size
    rows = -(-count // 16) * 16
    columns = np.zeros((window, window))
    columns[:, :count] = basis
    radius = (freq[:, None] ** 2 + freq[None, :] ** 2).astype(np.float64)
    weight = (9.0 * radius < window * window) * norm[:, None] * norm[None, :]
    angle = -PROPAGATION_COEF * (65536.0 / (window * window)) * radius
    prop = np.zeros((2, rows, window), np.float32)
    prop[0, :count, :count] = weight * np.cos(angle)
    prop[1, :count, :count] = weight * np.sin(angle)
    k = np.arange(window)
    f = np.where(k < window // 2, k, k - window)
    radius = (f[:, None] ** 2 + f[None, :] ** 2).astype(np.float64)
    inside = 16.0 * radius < window * window
    start = inside * (window / math.sqrt(inside.sum())) * np.exp(-1j * (DEFOCUS_COEF / window) * radius)
    wave = np.fft.ifft2(start) * window
    square = np.stack([columns, columns.T, wave.real, wave.imag]).astype(ml_dtypes.bfloat16)
    return square, prop


@functools.cache
def half_angle_coefs():
    nodes = 0.25 * (1.0 + np.cos(np.pi * (np.arange(400) + 0.5) / 400)) / 2.0
    f = np.sqrt(nodes)
    sin = np.polynomial.Polynomial.fit(nodes, math.sqrt(2.0) * np.sin(np.pi * f) / f, 4, domain=[0, 0.25], window=[0, 0.25]).coef
    cos = np.polynomial.Polynomial.fit(nodes, math.sqrt(2.0) * np.cos(np.pi * f), 4, domain=[0, 0.25], window=[0, 0.25]).coef
    return [float(c) for c in sin], [float(c) for c in cos]


def horner(coefs, z):
    total = coefs[-1]
    for c in coefs[-2::-1]:
        total = total * z + c
    return total


def cos_sin(phase):
    sin_coefs, cos_coefs = half_angle_coefs()
    turn = phase * (0.5 / math.pi)
    turn = turn - jnp.round(turn)
    z = turn * turn
    s = turn * horner(sin_coefs, z)
    c = horner(cos_coefs, z)
    return 1.0 - s * s, s * c


def dot(a, b):
    return jnp.dot(a, b, preferred_element_type=jnp.float32)


def kernel(
    n_lat, n_slc, window, field,
    xy_ref, species_ref, slab_ref, amp_ref, spread_ref, pos_ref, square_hbm, prop_hbm,
    out_ref,
    mine, recv, square, prop, table_sem, send_sem, recv_sem,
):
    bf16, f32 = jnp.bfloat16, jnp.float32
    t, u = lax.axis_index("lat"), lax.axis_index("slc")
    before, after = lax.rem(t + n_lat - 1, n_lat), lax.rem(t + 1, n_lat)
    owners = [lax.rem(u + n_slc - k, n_slc) for k in range(n_slc)]

    barrier = pltpu.get_barrier_semaphore()
    for k in range(n_slc):
        for lat in (before, after) if k == 0 else (before, after, t):
            pl.semaphore_signal(
                barrier, inc=1, device_id={"lat": lat, "slc": owners[k]}, device_id_type=MESH
            )
    loads = [
        pltpu.make_async_copy(square_hbm, square, table_sem.at[0]),
        pltpu.make_async_copy(prop_hbm, prop, table_sem.at[1]),
    ]
    for load in loads:
        load.start()

    species = species_ref[0]
    slab = slab_ref[0]
    amp = jnp.zeros(species.shape, f32)
    spread = jnp.ones(species.shape, f32)
    for i in range(amp_ref.shape[0]):
        amp = jnp.where(species == i, amp_ref[i], amp)
        spread = jnp.where(species == i, spread_ref[i], spread)
    layers = 2
    factor = (-0.5 * LOG2E) / (spread * spread)
    fields = [xy_ref[0, 0, 0:1, :], xy_ref[0, 0, 1:2, :], factor]
    fields += [jnp.where(slab == s, amp, 0.0) for s in range(layers)]
    for row, value in enumerate(fields):
        for h in range(2):
            mine[h, row : row + 1, :] = value[:, h * LANES : (h + 1) * LANES]
    for h in range(2):
        mine[h, len(fields) :, :] = jnp.zeros((8 - len(fields), LANES), f32)

    pl.semaphore_wait(barrier, 3 * n_slc - 1)
    sends = {}
    for k in range(n_slc):
        pieces = [(after, mine.at[1], recv.at[k, 0]), (before, mine.at[0], recv.at[k, 3])]
        if k > 0:
            pieces.append((t, mine, recv.at[k, 1:3]))
        for i, (lat, source, target) in enumerate(pieces):
            copy = pltpu.make_async_remote_copy(
                src_ref=source, dst_ref=target,
                send_sem=send_sem.at[k, i], recv_sem=recv_sem.at[k, i],
                device_id={"lat": lat, "slc": owners[k]}, device_id_type=MESH,
            )
            copy.start()
            sends[k, i] = copy
    for load in loads:
        load.wait()

    probes = pos_ref.shape[0]
    anchor_x = pos_ref[0, 0].astype(f32)
    anchor_y = [pos_ref[p, 1].astype(f32) for p in range(probes)]
    pixel = lax.broadcasted_iota(jnp.int32, (window, LANES), 0).astype(f32)
    half = 0.5 * window
    rows = prop.shape[1]
    basis, basis_t = square.at[0], square.at[1]

    waves = [(square[2].astype(f32), square[3].astype(f32))] * probes
    for k in range(n_slc):
        for i in range(2 if k == 0 else 3):
            sends[k, i].wait_recv()
        groups = [recv[k, 0], mine[0], mine[1], recv[k, 3]] if k == 0 else [recv[k, g] for g in range(4)]
        atoms, rel_x = None, None
        for group in groups[::-1]:
            rel = group[0:1, :] - anchor_x
            rel = jnp.where(rel < -0.5 * field, rel + field, rel)
            rel = jnp.where(rel >= 0.5 * field, rel - field, rel)
            if atoms is None:
                atoms, rel_x = group, rel
            else:
                seen = jnp.logical_and(rel >= -half, rel < window + half)
                atoms = jnp.where(seen, group, atoms)
                rel_x = jnp.where(seen, rel, rel_x)
        factor = atoms[2:3, :]
        d = rel_x - pixel
        across = jnp.exp2(d * d * factor).astype(bf16)
        along = []
        for p in range(probes):
            rel_y = atoms[1:2, :] - anchor_y[p]
            rel_y = jnp.where(rel_y < 0.0, rel_y + window, rel_y)
            e = jnp.abs(rel_y - pixel)
            e = jnp.minimum(e, window - e)
            along.append(jnp.exp2(e * e * factor))
        for s in range(layers):
            last = k == n_slc - 1 and s == layers - 1
            for p in range(probes):
                weighted = (atoms[3 + s : 4 + s, :] * along[p]).astype(bf16)
                phase = lax.dot_general(
                    across, weighted, (((1,), (1,)), ((), ())), preferred_element_type=f32
                )
                c, sn = cos_sin(phase)
                re, im = waves[p]
                sent = [(re * c - im * sn).astype(bf16), (re * sn + im * c).astype(bf16)]
                rowwise = [dot(w, basis[...]).astype(bf16) for w in sent]
                sr, si = [dot(basis_t[:rows, :], w) for w in rowwise]
                pr, pi = prop[0], prop[1]
                spectrum = [(sr * pr - si * pi).astype(bf16), (sr * pi + si * pr).astype(bf16)]
                back = [dot(w, basis_t[...]).astype(bf16) for w in spectrum]
                pad = jnp.zeros((window - rows, window), bf16)
                back = [jnp.concatenate([w, pad], 0) for w in back]
                waves[p] = tuple(dot(basis[...], w) for w in back)
                if last:
                    for part in range(2):
                        out_ref[p, part] = waves[p][part].astype(bf16)
    for copy in sends.values():
        copy.wait_send()


def solution(mesh):
    n_lat, n_slc = mesh.shape["lat"], mesh.shape["slc"]
    window = 256

    def shards(atom_xy, atom_species, atom_slab, species_amp, species_spread, margin, probe_pos):
        square, prop = tables(window)
        atoms = atom_xy.shape[-1]
        field = float(n_lat * atoms * 4)
        probes = probe_pos.shape[0]
        vmem = pl.BlockSpec(memory_space=pltpu.VMEM)
        smem = pl.BlockSpec(memory_space=pltpu.SMEM)
        hbm = pl.BlockSpec(memory_space=pl.ANY)
        out = pl.pallas_call(
            functools.partial(kernel, n_lat, n_slc, window, field),
            out_shape=jax.ShapeDtypeStruct((probes, 2, window, window), jnp.bfloat16),
            in_specs=[vmem, vmem, vmem, smem, smem, smem, hbm, hbm],
            out_specs=vmem,
            scratch_shapes=[
                pltpu.VMEM((2, 8, LANES), jnp.float32),
                pltpu.VMEM((n_slc, 4, 8, LANES), jnp.float32),
                pltpu.VMEM(square.shape, jnp.bfloat16),
                pltpu.VMEM(prop.shape, jnp.float32),
                pltpu.SemaphoreType.DMA((2,)),
                pltpu.SemaphoreType.DMA((n_slc, 3)),
                pltpu.SemaphoreType.DMA((n_slc, 3)),
            ],
            compiler_params=pltpu.CompilerParams(
                collective_id=0, has_side_effects=True, vmem_limit_bytes=40 * 2**20
            ),
            name="multislice",
        )(atom_xy, atom_species, atom_slab, species_amp, species_spread, probe_pos,
          jnp.asarray(square), jnp.asarray(prop))
        return jnp.transpose(out, (0, 2, 1, 3))

    in_specs = (
        P(("groups", "lat"), "slc", None, None),
        P(("groups", "lat"), "slc", None),
        P(("groups", "lat"), "slc", None),
        P(),
        P(),
        P(("groups", "lat"), "slc", None, "rep", None, None),
        P(("groups", "lat", "slc", "rep"), None),
    )
    out_specs = P(("groups", "lat", "slc", "rep"), None, None, None)
    return jax.shard_map(shards, mesh=mesh, in_specs=in_specs, out_specs=out_specs, check_vma=False)
```

```python
import functools
import math

import jax
import jax.numpy as jnp
import ml_dtypes
import numpy as np
from jax import lax
from jax.experimental import pallas as pl
from jax.experimental.pallas import tpu as pltpu
from jax.sharding import PartitionSpec as P

PROPAGATION_COEF = 0.001
DEFOCUS_COEF = 4.19
LOG2E = math.log2(math.e)
MESH = pl.DeviceIdType.MESH

LANES = 128
CHUNK = 64
LAG = 4
FILL = 1


def real_basis(window):
    top = max(k for k in range(window // 2) if 9 * k * k < window * window)
    freq = np.concatenate([np.arange(top + 1), np.arange(1, top + 1)])
    pixel = np.arange(window)
    angle = 2.0 * np.pi / window * (pixel[:, None] * freq[None, :] % window)
    basis = np.where(np.arange(freq.size) <= top, np.cos(angle), np.sin(angle))
    norm = np.where(freq == 0, 1.0, 2.0) / window
    return basis, freq, norm


@functools.cache
def tables(window):
    basis, freq, norm = real_basis(window)
    count = freq.size
    rows = -(-count // 16) * 16
    columns = np.zeros((window, window))
    columns[:, :count] = basis
    radius = (freq[:, None] ** 2 + freq[None, :] ** 2).astype(np.float64)
    weight = (9.0 * radius < window * window) * norm[:, None] * norm[None, :]
    angle = -PROPAGATION_COEF * (65536.0 / (window * window)) * radius
    prop = np.zeros((2, rows, window), np.float32)
    prop[0, :count, :count] = weight * np.cos(angle)
    prop[1, :count, :count] = weight * np.sin(angle)
    k = np.arange(window)
    f = np.where(k < window // 2, k, k - window)
    radius = (f[:, None] ** 2 + f[None, :] ** 2).astype(np.float64)
    inside = 16.0 * radius < window * window
    start = inside * (window / math.sqrt(inside.sum())) * np.exp(-1j * (DEFOCUS_COEF / window) * radius)
    wave = np.fft.ifft2(start) * window
    square = np.stack([columns, columns.T, wave.real, wave.imag]).astype(ml_dtypes.bfloat16)
    return square, prop


@functools.cache
def half_angle_coefs():
    nodes = 0.25 * (1.0 + np.cos(np.pi * (np.arange(400) + 0.5) / 400)) / 2.0
    f = np.sqrt(nodes)
    sin = np.polynomial.Polynomial.fit(nodes, math.sqrt(2.0) * np.sin(np.pi * f) / f, 4, domain=[0, 0.25], window=[0, 0.25]).coef
    cos = np.polynomial.Polynomial.fit(nodes, math.sqrt(2.0) * np.cos(np.pi * f), 4, domain=[0, 0.25], window=[0, 0.25]).coef
    return [float(c) for c in sin], [float(c) for c in cos]


def horner(coefs, z):
    total = coefs[-1]
    for c in coefs[-2::-1]:
        total = total * z + c
    return total


def cos_sin(phase):
    sin_coefs, cos_coefs = half_angle_coefs()
    turn = phase * (0.5 / math.pi)
    turn = turn - jnp.round(turn)
    z = turn * turn
    s = turn * horner(sin_coefs, z)
    c = horner(cos_coefs, z)
    return 1.0 - s * s, s * c


def dot(a, b):
    return jnp.dot(a, b, preferred_element_type=jnp.float32)


def kernel(
    n_lat, n_slc, window, field,
    xy_hbm, species_hbm, slab_hbm, amp_hbm, spread_hbm, pos_hbm, square_hbm, prop_hbm,
    out_ref,
    xy_ref, species_ref, slab_ref, amp_ref, spread_ref, pos_ref, square, prop,
    mine, recv, across, weighted, turn, sent, mixed, spectrum,
    load_sem, send_sem, recv_sem,
):
    bf16, f32 = jnp.bfloat16, jnp.float32
    t, u = lax.axis_index("lat"), lax.axis_index("slc")
    before, after = lax.rem(t + n_lat - 1, n_lat), lax.rem(t + 1, n_lat)
    owners = [lax.rem(u + n_slc - k, n_slc) for k in range(n_slc)]

    barrier = pltpu.get_barrier_semaphore()
    for k in range(n_slc):
        for lat in (before, after) if k == 0 else (before, after, t):
            pl.semaphore_signal(
                barrier, inc=1, device_id={"lat": lat, "slc": owners[k]}, device_id_type=MESH
            )
    pairs = [
        (xy_hbm, xy_ref), (species_hbm, species_ref), (slab_hbm, slab_ref), (amp_hbm, amp_ref),
        (spread_hbm, spread_ref), (pos_hbm, pos_ref), (square_hbm, square), (prop_hbm, prop),
    ]
    loads = [pltpu.make_async_copy(*pair, load_sem.at[i]) for i, pair in enumerate(pairs)]
    for load in loads:
        load.start()
    for load in loads[:5]:
        load.wait()

    species = species_ref[0]
    slab = slab_ref[0]
    amp = jnp.zeros(species.shape, f32)
    spread = jnp.ones(species.shape, f32)
    for i in range(amp_ref.shape[0]):
        amp = jnp.where(species == i, amp_ref[i], amp)
        spread = jnp.where(species == i, spread_ref[i], spread)
    layers = 2
    factor = (-0.5 * LOG2E) / (spread * spread)
    fields = [xy_ref[0, 0, 0:1, :], xy_ref[0, 0, 1:2, :], factor]
    fields += [jnp.where(slab == s, amp, 0.0) for s in range(layers)]
    for row, value in enumerate(fields):
        for h in range(2):
            mine[h, row : row + 1, :] = value[:, h * LANES : (h + 1) * LANES]
    for h in range(2):
        mine[h, len(fields) :, :] = jnp.zeros((8 - len(fields), LANES), f32)

    pl.semaphore_wait(barrier, 3 * n_slc - 1)
    sends = {}
    for k in range(n_slc):
        pieces = [(after, mine.at[1], recv.at[k, 0]), (before, mine.at[0], recv.at[k, 3])]
        if k > 0:
            pieces.append((t, mine, recv.at[k, 1:3]))
        for i, (lat, source, target) in enumerate(pieces):
            copy = pltpu.make_async_remote_copy(
                src_ref=source, dst_ref=target,
                send_sem=send_sem.at[k, i], recv_sem=recv_sem.at[k, i],
                device_id={"lat": lat, "slc": owners[k]}, device_id_type=MESH,
            )
            copy.start()
            sends[k, i] = copy
    for load in loads[5:]:
        load.wait()

    probes = pos_ref.shape[0]
    anchor_x = pos_ref[0, 0].astype(f32)
    anchor_y = [pos_ref[p, 1].astype(f32) for p in range(probes)]
    pixel = lax.broadcasted_iota(jnp.int32, (window, LANES), 0).astype(f32)
    half = 0.5 * window
    rows = prop.shape[1]
    basis, basis_t = square.at[0], square.at[1]
    steps = n_slc * layers
    done = {}

    def owner_atoms(k):
        for i in range(2 if k == 0 else 3):
            sends[k, i].wait_recv()
        groups = [recv[k, 0], mine[0], mine[1], recv[k, 3]] if k == 0 else [recv[k, g] for g in range(4)]
        atoms, rel_x = None, None
        for group in groups[::-1]:
            rel = group[0:1, :] - anchor_x
            rel = jnp.where(rel < -0.5 * field, rel + field, rel)
            rel = jnp.where(rel >= 0.5 * field, rel - field, rel)
            if atoms is None:
                atoms, rel_x = group, rel
            else:
                seen = jnp.logical_and(rel >= -half, rel < window + half)
                atoms = jnp.where(seen, group, atoms)
                rel_x = jnp.where(seen, rel, rel_x)
        return atoms, rel_x

    def phases():
        for k in range(n_slc):
            atoms, rel_x = owner_atoms(k)
            factor = atoms[2:3, :]
            d = rel_x - pixel
            across[...] = jnp.exp2(d * d * factor).astype(bf16)
            for p in range(probes):
                rel_y = atoms[1:2, :] - anchor_y[p]
                rel_y = jnp.where(rel_y < 0.0, rel_y + window, rel_y)
                e = jnp.abs(rel_y - pixel)
                e = jnp.minimum(e, window - e)
                along = jnp.exp2(e * e * factor)
                for s in range(layers):
                    weighted[s, p] = (atoms[3 + s : 4 + s, :] * along).astype(bf16)
            for s in range(layers):
                for p in range(probes):
                    phase = lax.dot_general(
                        across[...], weighted[s, p], (((1,), (1,)), ((), ())), preferred_element_type=f32
                    )
                    step = k * layers + s
                    for r in range(0, window, CHUNK):
                        c, sn = cos_sin(phase[r : r + CHUNK])
                        turn[step, p, 0, r : r + CHUNK, :] = c
                        turn[step, p, 1, r : r + CHUNK, :] = sn
                        if r + CHUNK == window:
                            done[step, p] = True
                        yield

    blocks = [(r, min(96, rows - r)) for r in range(0, rows, 96)]

    def chain(p):
        wave = (square[2].astype(f32), square[3].astype(f32))
        for step in range(steps):
            yield step
            for r in range(0, window, CHUNK):
                part = slice(r, r + CHUNK)
                re, im = wave[0][part], wave[1][part]
                c, sn = turn[step, p, 0, part, :], turn[step, p, 1, part, :]
                sent[p, 0, part, :] = (re * c - im * sn).astype(bf16)
                sent[p, 1, part, :] = (re * sn + im * c).astype(bf16)
            yield
            for plane in range(2):
                value = dot(basis_t[:rows, :], sent[p, plane]).astype(bf16)
                for r, size in blocks:
                    start = 2 * r + plane * size
                    mixed[p, start : start + size, :] = value[r : r + size]
                yield
            for r, size in blocks:
                both = dot(mixed[p, 2 * r : 2 * (r + size), :], basis[...])
                sr, si = both[:size], both[size:]
                pr, pi = prop[0, r : r + size, :], prop[1, r : r + size, :]
                spectrum[p, r : r + size, :] = (sr * pr - si * pi).astype(bf16)
                spectrum[p, rows + r : rows + r + size, :] = (sr * pi + si * pr).astype(bf16)
                yield
            back = dot(spectrum[p], basis_t[...]).astype(bf16)
            yield
            pad = jnp.zeros((window - rows, window), bf16)
            wave = []
            for plane in range(2):
                full = jnp.concatenate([back[plane * rows : (plane + 1) * rows], pad], 0)
                wave.append(dot(basis[...], full))
                if step == steps - 1:
                    out_ref[p, plane] = wave[plane].astype(bf16)
                yield

    filler = phases()
    chains = [chain(p) for p in range(probes)]
    at = [0] * probes
    live = list(range(probes))
    count = 0
    while live:
        for p in list(live):
            if count < p * LAG:
                continue
            mark = next(chains[p], "end")
            if mark == "end":
                live.remove(p)
            elif mark is not None:
                while (mark, p) not in done:
                    next(filler)
            for _ in range(FILL):
                next(filler, None)
        count += 1
    for copy in sends.values():
        copy.wait_send()


def solution(mesh):
    n_lat, n_slc = mesh.shape["lat"], mesh.shape["slc"]
    window = 256

    def shards(atom_xy, atom_species, atom_slab, species_amp, species_spread, margin, probe_pos):
        square, prop = tables(window)
        atoms = atom_xy.shape[-1]
        field = float(n_lat * atoms * 4)
        probes = probe_pos.shape[0]
        vmem = pl.BlockSpec(memory_space=pltpu.VMEM)
        hbm = pl.BlockSpec(memory_space=pltpu.HBM)
        rows = prop.shape[1]
        layers = 2
        out = pl.pallas_call(
            functools.partial(kernel, n_lat, n_slc, window, field),
            out_shape=jax.ShapeDtypeStruct((probes, 2, window, window), jnp.bfloat16),
            in_specs=[hbm] * 8,
            out_specs=vmem,
            scratch_shapes=[
                pltpu.VMEM(atom_xy.shape, jnp.float32),
                pltpu.VMEM(atom_species.shape, jnp.int32),
                pltpu.VMEM(atom_slab.shape, jnp.int32),
                pltpu.SMEM(species_amp.shape, jnp.float32),
                pltpu.SMEM(species_spread.shape, jnp.float32),
                pltpu.SMEM(probe_pos.shape, jnp.int32),
                pltpu.VMEM(square.shape, jnp.bfloat16),
                pltpu.VMEM(prop.shape, jnp.float32),
                pltpu.VMEM((2, 8, LANES), jnp.float32),
                pltpu.VMEM((n_slc, 4, 8, LANES), jnp.float32),
                pltpu.VMEM((window, LANES), jnp.bfloat16),
                pltpu.VMEM((layers, probes, window, LANES), jnp.bfloat16),
                pltpu.VMEM((n_slc * layers, probes, 2, window, window), jnp.float32),
                pltpu.VMEM((probes, 2, window, window), jnp.bfloat16),
                pltpu.VMEM((probes, 2 * rows, window), jnp.bfloat16),
                pltpu.VMEM((probes, 2 * rows, window), jnp.bfloat16),
                pltpu.SemaphoreType.DMA((8,)),
                pltpu.SemaphoreType.DMA((n_slc, 3)),
                pltpu.SemaphoreType.DMA((n_slc, 3)),
            ],
            compiler_params=pltpu.CompilerParams(
                collective_id=0, has_side_effects=True, vmem_limit_bytes=63 * 2**20
            ),
            name="multislice",
        )(atom_xy, atom_species, atom_slab, species_amp, species_spread, probe_pos,
          jnp.asarray(square), jnp.asarray(prop))
        return jnp.transpose(out, (0, 2, 1, 3))

    in_specs = (
        P(("groups", "lat"), "slc", None, None),
        P(("groups", "lat"), "slc", None),
        P(("groups", "lat"), "slc", None),
        P(),
        P(),
        P(("groups", "lat"), "slc", None, "rep", None, None),
        P(("groups", "lat", "slc", "rep"), None),
    )
    out_specs = P(("groups", "lat", "slc", "rep"), None, None, None)
    return jax.shard_map(shards, mesh=mesh, in_specs=in_specs, out_specs=out_specs, check_vma=False)
```

```python
import functools
import math

import jax
import jax.numpy as jnp
import ml_dtypes
import numpy as np
from jax import lax
from jax.experimental import pallas as pl
from jax.experimental.pallas import tpu as pltpu
from jax.sharding import PartitionSpec as P

PROPAGATION_COEF = 0.001
DEFOCUS_COEF = 4.19
LOG2E = math.log2(math.e)
MESH = pl.DeviceIdType.MESH

LANES = 128
CHUNK = 64
LAG = 4
FILL = 1


def real_basis(window):
    top = max(k for k in range(window // 2) if 9 * k * k < window * window)
    freq = np.concatenate([np.arange(top + 1), np.arange(1, top + 1)])
    pixel = np.arange(window)
    angle = 2.0 * np.pi / window * (pixel[:, None] * freq[None, :] % window)
    basis = np.where(np.arange(freq.size) <= top, np.cos(angle), np.sin(angle))
    norm = np.where(freq == 0, 1.0, 2.0) / window
    return basis, freq, norm


@functools.cache
def tables(window):
    basis, freq, norm = real_basis(window)
    count = freq.size
    rows = -(-count // 16) * 16
    columns = np.zeros((window, window))
    columns[:, :count] = basis
    radius = (freq[:, None] ** 2 + freq[None, :] ** 2).astype(np.float64)
    weight = (9.0 * radius < window * window) * norm[:, None] * norm[None, :]
    angle = -PROPAGATION_COEF * (65536.0 / (window * window)) * radius
    prop = np.zeros((2, rows, window), np.float32)
    prop[0, :count, :count] = weight * np.cos(angle)
    prop[1, :count, :count] = weight * np.sin(angle)
    k = np.arange(window)
    f = np.where(k < window // 2, k, k - window)
    radius = (f[:, None] ** 2 + f[None, :] ** 2).astype(np.float64)
    inside = 16.0 * radius < window * window
    start = inside * (window / math.sqrt(inside.sum())) * np.exp(-1j * (DEFOCUS_COEF / window) * radius)
    wave = np.fft.ifft2(start) * window
    square = np.stack([columns, columns.T, wave.real, wave.imag]).astype(ml_dtypes.bfloat16)
    return square, prop


@functools.cache
def half_angle_coefs():
    nodes = 0.25 * (1.0 + np.cos(np.pi * (np.arange(400) + 0.5) / 400)) / 2.0
    f = np.sqrt(nodes)
    sin = np.polynomial.Polynomial.fit(nodes, math.sqrt(2.0) * np.sin(np.pi * f) / f, 4, domain=[0, 0.25], window=[0, 0.25]).coef
    cos = np.polynomial.Polynomial.fit(nodes, math.sqrt(2.0) * np.cos(np.pi * f), 4, domain=[0, 0.25], window=[0, 0.25]).coef
    return [float(c) for c in sin], [float(c) for c in cos]


def horner(coefs, z):
    total = coefs[-1]
    for c in coefs[-2::-1]:
        total = total * z + c
    return total


def cos_sin(phase):
    sin_coefs, cos_coefs = half_angle_coefs()
    turn = phase * (0.5 / math.pi)
    turn = turn - jnp.round(turn)
    z = turn * turn
    s = turn * horner(sin_coefs, z)
    c = horner(cos_coefs, z)
    return 1.0 - s * s, s * c


def dot(a, b):
    return jnp.dot(a, b, preferred_element_type=jnp.float32)


def kernel(
    n_lat, n_slc, window, field,
    xy_hbm, species_hbm, slab_hbm, amp_hbm, spread_hbm, pos_hbm, square_hbm, prop_hbm,
    out_ref,
    amp_ref, spread_ref, pos_ref, square, prop, xy_side, xy_mid, ids_side, ids_mid,
    across, weighted, turn, sent, mixed, spectrum,
    load_sem, send_sem, recv_sem,
):
    bf16, f32 = jnp.bfloat16, jnp.float32
    t, u = lax.axis_index("lat"), lax.axis_index("slc")
    before, after = lax.rem(t + n_lat - 1, n_lat), lax.rem(t + 1, n_lat)
    owners = [lax.rem(u + n_slc - k, n_slc) for k in range(n_slc)]

    barrier = pltpu.get_barrier_semaphore()
    for k in range(n_slc):
        for lat in (before, after) if k == 0 else (before, after, t):
            pl.semaphore_signal(
                barrier, inc=1, device_id={"lat": lat, "slc": owners[k]}, device_id_type=MESH
            )
    pairs = [
        (xy_hbm.at[0, 0], xy_mid.at[0]), (species_hbm.at[0], ids_mid.at[0, 0]),
        (slab_hbm.at[0], ids_mid.at[0, 1]), (amp_hbm, amp_ref), (spread_hbm, spread_ref),
        (pos_hbm, pos_ref), (square_hbm, square), (prop_hbm, prop),
    ]
    loads = [pltpu.make_async_copy(*pair, load_sem.at[i]) for i, pair in enumerate(pairs)]
    for load in loads:
        load.start()

    layers = 2
    low, high = pl.ds(0, LANES), pl.ds(LANES, LANES)
    pl.semaphore_wait(barrier, 3 * n_slc - 1)
    sends = {}
    for k in range(n_slc):
        for side, (lat, part) in enumerate([(after, high), (before, low), (t, pl.ds(0, 2 * LANES))]):
            if side == 2 and k == 0:
                continue
            if side < 2:
                targets = [xy_side.at[k, side], ids_side.at[k, side, 0], ids_side.at[k, side, 1]]
            else:
                targets = [xy_mid.at[k], ids_mid.at[k, 0], ids_mid.at[k, 1]]
            sources = [xy_hbm.at[0, 0, :, part], species_hbm.at[0, :, part], slab_hbm.at[0, :, part]]
            for i in range(3):
                copy = pltpu.make_async_remote_copy(
                    src_ref=sources[i], dst_ref=targets[i],
                    send_sem=send_sem.at[k, side, i], recv_sem=recv_sem.at[k, side, i],
                    device_id={"lat": lat, "slc": owners[k]}, device_id_type=MESH,
                )
                copy.start()
                sends[k, side, i] = copy
    for load in loads:
        load.wait()

    probes = pos_ref.shape[0]
    anchor_x = pos_ref[0, 0].astype(f32)
    anchor_y = [pos_ref[p, 1].astype(f32) for p in range(probes)]
    pixel = lax.broadcasted_iota(jnp.int32, (window, LANES), 0).astype(f32)
    half = 0.5 * window
    rows = prop.shape[1]
    basis, basis_t = square.at[0], square.at[1]
    steps = n_slc * layers
    done = {}

    def owner_atoms(k):
        for side in range(2 if k == 0 else 3):
            for i in range(3):
                sends[k, side, i].wait_recv()
        ends = [
            [xy_side[k, side, 0:1, :], xy_side[k, side, 1:2, :], ids_side[k, side, 0], ids_side[k, side, 1]]
            for side in range(2)
        ]
        middle = [
            [xy_mid[k, 0:1, h], xy_mid[k, 1:2, h], ids_mid[k, 0, :, h], ids_mid[k, 1, :, h]]
            for h in (low, high)
        ]
        atoms, rel_x = None, None
        for group in [ends[1], middle[1], middle[0], ends[0]]:
            rel = group[0] - anchor_x
            rel = jnp.where(rel < -0.5 * field, rel + field, rel)
            rel = jnp.where(rel >= 0.5 * field, rel - field, rel)
            if atoms is None:
                atoms, rel_x = group[1:], rel
            else:
                seen = jnp.logical_and(rel >= -half, rel < window + half)
                atoms = [jnp.where(seen, new, old) for new, old in zip(group[1:], atoms)]
                rel_x = jnp.where(seen, rel, rel_x)
        y, species, slab = atoms
        amp = jnp.zeros(species.shape, f32)
        spread = jnp.ones(species.shape, f32)
        for i in range(amp_ref.shape[0]):
            amp = jnp.where(species == i, amp_ref[i], amp)
            spread = jnp.where(species == i, spread_ref[i], spread)
        factor = (-0.5 * LOG2E) / (spread * spread)
        return rel_x, y, factor, [jnp.where(slab == s, amp, 0.0) for s in range(layers)]

    def phases():
        for k in range(n_slc):
            rel_x, y, factor, amps = owner_atoms(k)
            d = rel_x - pixel
            across[...] = jnp.exp2(d * d * factor).astype(bf16)
            for p in range(probes):
                rel_y = y - anchor_y[p]
                rel_y = jnp.where(rel_y < 0.0, rel_y + window, rel_y)
                e = jnp.abs(rel_y - pixel)
                e = jnp.minimum(e, window - e)
                along = jnp.exp2(e * e * factor)
                for s in range(layers):
                    weighted[s, p] = (amps[s] * along).astype(bf16)
            for s in range(layers):
                for p in range(probes):
                    phase = lax.dot_general(
                        across[...], weighted[s, p], (((1,), (1,)), ((), ())), preferred_element_type=f32
                    )
                    step = k * layers + s
                    for r in range(0, window, CHUNK):
                        c, sn = cos_sin(phase[r : r + CHUNK])
                        turn[step, p, 0, r : r + CHUNK, :] = c
                        turn[step, p, 1, r : r + CHUNK, :] = sn
                        if r + CHUNK == window:
                            done[step, p] = True
                        yield

    blocks = [(r, min(96, rows - r)) for r in range(0, rows, 96)]

    def chain(p):
        wave = (square[2].astype(f32), square[3].astype(f32))
        for step in range(steps):
            yield step
            for r in range(0, window, CHUNK):
                part = slice(r, r + CHUNK)
                re, im = wave[0][part], wave[1][part]
                c, sn = turn[step, p, 0, part, :], turn[step, p, 1, part, :]
                sent[p, 0, part, :] = (re * c - im * sn).astype(bf16)
                sent[p, 1, part, :] = (re * sn + im * c).astype(bf16)
            yield
            for plane in range(2):
                value = dot(basis_t[:rows, :], sent[p, plane]).astype(bf16)
                for r, size in blocks:
                    start = 2 * r + plane * size
                    mixed[p, start : start + size, :] = value[r : r + size]
                yield
            for r, size in blocks:
                both = dot(mixed[p, 2 * r : 2 * (r + size), :], basis[...])
                sr, si = both[:size], both[size:]
                pr, pi = prop[0, r : r + size, :], prop[1, r : r + size, :]
                spectrum[p, r : r + size, :] = (sr * pr - si * pi).astype(bf16)
                spectrum[p, rows + r : rows + r + size, :] = (sr * pi + si * pr).astype(bf16)
                yield
            back = dot(spectrum[p], basis_t[...]).astype(bf16)
            yield
            pad = jnp.zeros((window - rows, window), bf16)
            wave = []
            for plane in range(2):
                full = jnp.concatenate([back[plane * rows : (plane + 1) * rows], pad], 0)
                wave.append(dot(basis[...], full))
                if step == steps - 1:
                    out_ref[p, plane] = wave[plane].astype(bf16)
                yield

    filler = phases()
    chains = [chain(p) for p in range(probes)]
    at = [0] * probes
    live = list(range(probes))
    count = 0
    while live:
        for p in list(live):
            if count < p * LAG:
                continue
            mark = next(chains[p], "end")
            if mark == "end":
                live.remove(p)
            elif mark is not None:
                while (mark, p) not in done:
                    next(filler)
            for _ in range(FILL):
                next(filler, None)
        count += 1
    for copy in sends.values():
        copy.wait_send()


def solution(mesh):
    n_lat, n_slc = mesh.shape["lat"], mesh.shape["slc"]
    window = 256

    def shards(atom_xy, atom_species, atom_slab, species_amp, species_spread, margin, probe_pos):
        square, prop = tables(window)
        atoms = atom_xy.shape[-1]
        field = float(n_lat * atoms * 4)
        probes = probe_pos.shape[0]
        vmem = pl.BlockSpec(memory_space=pltpu.VMEM)
        hbm = pl.BlockSpec(memory_space=pltpu.HBM)
        rows = prop.shape[1]
        layers = 2
        out = pl.pallas_call(
            functools.partial(kernel, n_lat, n_slc, window, field),
            out_shape=pltpu.VMEM((probes, 2, window, window), jnp.bfloat16),
            in_specs=[hbm] * 8,
            out_specs=vmem,
            scratch_shapes=[
                pltpu.SMEM(species_amp.shape, jnp.float32),
                pltpu.SMEM(species_spread.shape, jnp.float32),
                pltpu.SMEM(probe_pos.shape, jnp.int32),
                pltpu.VMEM(square.shape, jnp.bfloat16),
                pltpu.VMEM(prop.shape, jnp.float32),
                pltpu.VMEM((n_slc, 2, 2, LANES), jnp.float32),
                pltpu.VMEM((n_slc, 2, 2 * LANES), jnp.float32),
                pltpu.VMEM((n_slc, 2, 2, 1, LANES), jnp.int32),
                pltpu.VMEM((n_slc, 2, 1, 2 * LANES), jnp.int32),
                pltpu.VMEM((window, LANES), jnp.bfloat16),
                pltpu.VMEM((layers, probes, window, LANES), jnp.bfloat16),
                pltpu.VMEM((n_slc * layers, probes, 2, window, window), jnp.float32),
                pltpu.VMEM((probes, 2, window, window), jnp.bfloat16),
                pltpu.VMEM((probes, 2 * rows, window), jnp.bfloat16),
                pltpu.VMEM((probes, 2 * rows, window), jnp.bfloat16),
                pltpu.SemaphoreType.DMA((8,)),
                pltpu.SemaphoreType.DMA((n_slc, 3, 3)),
                pltpu.SemaphoreType.DMA((n_slc, 3, 3)),
            ],
            compiler_params=pltpu.CompilerParams(
                collective_id=0, has_side_effects=True, vmem_limit_bytes=int(63.4 * 2**20)
            ),
            name="multislice",
        )(atom_xy, atom_species, atom_slab, species_amp, species_spread, probe_pos,
          jnp.asarray(square), jnp.asarray(prop))
        return jnp.transpose(out, (0, 2, 1, 3))

    in_specs = (
        P(("groups", "lat"), "slc", None, None),
        P(("groups", "lat"), "slc", None),
        P(("groups", "lat"), "slc", None),
        P(),
        P(),
        P(("groups", "lat"), "slc", None, "rep", None, None),
        P(("groups", "lat", "slc", "rep"), None),
    )
    out_specs = P(("groups", "lat", "slc", "rep"), None, None, None)
    return jax.shard_map(shards, mesh=mesh, in_specs=in_specs, out_specs=out_specs, check_vma=False)
```

```python
import functools
import math

import jax
import jax.numpy as jnp
import ml_dtypes
import numpy as np
from jax import lax
from jax.experimental import pallas as pl
from jax.experimental.pallas import tpu as pltpu
from jax.sharding import PartitionSpec as P

PROPAGATION_COEF = 0.001
DEFOCUS_COEF = 4.19
LOG2E = math.log2(math.e)
MESH = pl.DeviceIdType.MESH

LANES = 128
CHUNK = 64
LAG = 4
PERIOD = 3


def real_basis(window):
    top = max(k for k in range(window // 2) if 9 * k * k < window * window)
    freq = np.concatenate([np.arange(top + 1), np.arange(1, top + 1)])
    pixel = np.arange(window)
    angle = 2.0 * np.pi / window * (pixel[:, None] * freq[None, :] % window)
    basis = np.where(np.arange(freq.size) <= top, np.cos(angle), np.sin(angle))
    norm = np.where(freq == 0, 1.0, 2.0) / window
    return basis, freq, norm


@functools.cache
def tables(window):
    basis, freq, norm = real_basis(window)
    count = freq.size
    rows = -(-count // 16) * 16
    columns = np.zeros((window, window))
    columns[:, :count] = basis
    radius = (freq[:, None] ** 2 + freq[None, :] ** 2).astype(np.float64)
    weight = (9.0 * radius < window * window) * norm[:, None] * norm[None, :]
    angle = -PROPAGATION_COEF * (65536.0 / (window * window)) * radius
    prop = np.zeros((2, rows, window), np.float32)
    prop[0, :count, :count] = weight * np.cos(angle)
    prop[1, :count, :count] = weight * np.sin(angle)
    k = np.arange(window)
    f = np.where(k < window // 2, k, k - window)
    radius = (f[:, None] ** 2 + f[None, :] ** 2).astype(np.float64)
    inside = 16.0 * radius < window * window
    start = inside * (window / math.sqrt(inside.sum())) * np.exp(-1j * (DEFOCUS_COEF / window) * radius)
    wave = np.fft.ifft2(start) * window
    square = np.stack([columns, columns.T, wave.real, wave.imag]).astype(ml_dtypes.bfloat16)
    return square, prop


@functools.cache
def half_angle_coefs():
    nodes = 0.25 * (1.0 + np.cos(np.pi * (np.arange(400) + 0.5) / 400)) / 2.0
    f = np.sqrt(nodes)
    sin = np.polynomial.Polynomial.fit(nodes, math.sqrt(2.0) * np.sin(np.pi * f) / f, 4, domain=[0, 0.25], window=[0, 0.25]).coef
    cos = np.polynomial.Polynomial.fit(nodes, math.sqrt(2.0) * np.cos(np.pi * f), 4, domain=[0, 0.25], window=[0, 0.25]).coef
    return [float(c) for c in sin], [float(c) for c in cos]


def horner(coefs, z):
    total = coefs[-1]
    for c in coefs[-2::-1]:
        total = total * z + c
    return total


def cos_sin(phase):
    sin_coefs, cos_coefs = half_angle_coefs()
    turn = phase * (0.5 / math.pi)
    turn = turn - jnp.round(turn)
    z = turn * turn
    s = turn * horner(sin_coefs, z)
    c = horner(cos_coefs, z)
    return 1.0 - s * s, s * c


def dot(a, b):
    return jnp.dot(a, b, preferred_element_type=jnp.float32)


def kernel(
    n_lat, n_slc, window, field,
    xy_hbm, species_hbm, slab_hbm, amp_hbm, spread_hbm, pos_hbm, square_hbm, prop_hbm,
    out_ref,
    amp_ref, spread_ref, pos_ref, square, prop, xy_side, xy_mid, ids_side, ids_mid,
    across, weighted, turn, sent, mixed, spectrum,
    load_sem, send_sem, recv_sem,
):
    bf16, f32 = jnp.bfloat16, jnp.float32
    t, u = lax.axis_index("lat"), lax.axis_index("slc")
    before, after = lax.rem(t + n_lat - 1, n_lat), lax.rem(t + 1, n_lat)
    owners = [lax.rem(u + n_slc - k, n_slc) for k in range(n_slc)]

    barrier = pltpu.get_barrier_semaphore()
    for k in range(n_slc):
        for lat in (before, after) if k == 0 else (before, after, t):
            pl.semaphore_signal(
                barrier, inc=1, device_id={"lat": lat, "slc": owners[k]}, device_id_type=MESH
            )
    pairs = [
        (xy_hbm.at[0, 0], xy_mid.at[0]), (species_hbm.at[0], ids_mid.at[0, 0]),
        (slab_hbm.at[0], ids_mid.at[0, 1]), (amp_hbm, amp_ref), (spread_hbm, spread_ref),
        (pos_hbm, pos_ref), (square_hbm, square), (prop_hbm, prop),
    ]
    loads = [pltpu.make_async_copy(*pair, load_sem.at[i]) for i, pair in enumerate(pairs)]
    for load in loads:
        load.start()

    layers = 2
    low, high = pl.ds(0, LANES), pl.ds(LANES, LANES)
    pl.semaphore_wait(barrier, 3 * n_slc - 1)
    sends = {}
    for k in range(n_slc):
        for side, (lat, part) in enumerate([(after, high), (before, low), (t, pl.ds(0, 2 * LANES))]):
            if side == 2 and k == 0:
                continue
            if side < 2:
                targets = [xy_side.at[k, side], ids_side.at[k, side, 0], ids_side.at[k, side, 1]]
            else:
                targets = [xy_mid.at[k], ids_mid.at[k, 0], ids_mid.at[k, 1]]
            sources = [xy_hbm.at[0, 0, :, part], species_hbm.at[0, :, part], slab_hbm.at[0, :, part]]
            for i in range(3):
                copy = pltpu.make_async_remote_copy(
                    src_ref=sources[i], dst_ref=targets[i],
                    send_sem=send_sem.at[k, side, i], recv_sem=recv_sem.at[k, side, i],
                    device_id={"lat": lat, "slc": owners[k]}, device_id_type=MESH,
                )
                copy.start()
                sends[k, side, i] = copy
    for load in loads[:6]:
        load.wait()

    probes = pos_ref.shape[0]
    anchor_x = pos_ref[0, 0].astype(f32)
    anchor_y = [pos_ref[p, 1].astype(f32) for p in range(probes)]
    pixel = lax.broadcasted_iota(jnp.int32, (window, LANES), 0).astype(f32)
    half = 0.5 * window
    rows = prop.shape[1]
    basis, basis_t = square.at[0], square.at[1]
    steps = n_slc * layers
    done = {}

    def owner_atoms(k):
        for side in range(2 if k == 0 else 3):
            for i in range(3):
                sends[k, side, i].wait_recv()
        ends = [
            [xy_side[k, side, 0:1, :], xy_side[k, side, 1:2, :], ids_side[k, side, 0], ids_side[k, side, 1]]
            for side in range(2)
        ]
        middle = [
            [xy_mid[k, 0:1, h], xy_mid[k, 1:2, h], ids_mid[k, 0, :, h], ids_mid[k, 1, :, h]]
            for h in (low, high)
        ]
        atoms, rel_x = None, None
        for group in [ends[1], middle[1], middle[0], ends[0]]:
            rel = group[0] - anchor_x
            rel = jnp.where(rel < -0.5 * field, rel + field, rel)
            rel = jnp.where(rel >= 0.5 * field, rel - field, rel)
            if atoms is None:
                atoms, rel_x = group[1:], rel
            else:
                seen = jnp.logical_and(rel >= -half, rel < window + half)
                atoms = [jnp.where(seen, new, old) for new, old in zip(group[1:], atoms)]
                rel_x = jnp.where(seen, rel, rel_x)
        y, species, slab = atoms
        amp = jnp.zeros(species.shape, f32)
        spread = jnp.ones(species.shape, f32)
        for i in range(amp_ref.shape[0]):
            amp = jnp.where(species == i, amp_ref[i], amp)
            spread = jnp.where(species == i, spread_ref[i], spread)
        factor = (-0.5 * LOG2E) / (spread * spread)
        return rel_x, y, factor, [jnp.where(slab == s, amp, 0.0) for s in range(layers)]

    def phases():
        for k in range(n_slc):
            rel_x, y, factor, amps = owner_atoms(k)
            d = rel_x - pixel
            across[...] = jnp.exp2(d * d * factor).astype(bf16)
            for p in range(probes):
                rel_y = y - anchor_y[p]
                rel_y = jnp.where(rel_y < 0.0, rel_y + window, rel_y)
                e = jnp.abs(rel_y - pixel)
                e = jnp.minimum(e, window - e)
                along = jnp.exp2(e * e * factor)
                for s in range(layers):
                    weighted[s, p] = (amps[s] * along).astype(bf16)
            for s in range(layers):
                for p in range(probes):
                    phase = lax.dot_general(
                        across[...], weighted[s, p], (((1,), (1,)), ((), ())), preferred_element_type=f32
                    )
                    step = k * layers + s
                    for r in range(0, window, CHUNK):
                        c, sn = cos_sin(phase[r : r + CHUNK])
                        turn[step, p, 0, r : r + CHUNK, :] = c
                        turn[step, p, 1, r : r + CHUNK, :] = sn
                        if r + CHUNK == window:
                            done[step, p] = True
                        yield

    blocks = [(r, min(96, rows - r)) for r in range(0, rows, 96)]

    def chain(p):
        for step in range(steps):
            yield step
            if step == 0:
                if p == 0:
                    for load in loads[6:]:
                        load.wait()
                wave = (square[2].astype(f32), square[3].astype(f32))
            for r in range(0, window, CHUNK):
                part = slice(r, r + CHUNK)
                re, im = wave[0][part], wave[1][part]
                c, sn = turn[step, p, 0, part, :], turn[step, p, 1, part, :]
                sent[p, 0, part, :] = (re * c - im * sn).astype(bf16)
                sent[p, 1, part, :] = (re * sn + im * c).astype(bf16)
            yield
            for plane in range(2):
                value = dot(basis_t[:rows, :], sent[p, plane]).astype(bf16)
                for r, size in blocks:
                    start = 2 * r + plane * size
                    mixed[p, start : start + size, :] = value[r : r + size]
                yield
            for r, size in blocks:
                both = dot(mixed[p, 2 * r : 2 * (r + size), :], basis[...])
                sr, si = both[:size], both[size:]
                pr, pi = prop[0, r : r + size, :], prop[1, r : r + size, :]
                spectrum[p, r : r + size, :] = (sr * pr - si * pi).astype(bf16)
                spectrum[p, rows + r : rows + r + size, :] = (sr * pi + si * pr).astype(bf16)
                yield
            back = dot(spectrum[p], basis_t[...]).astype(bf16)
            yield
            pad = jnp.zeros((window - rows, window), bf16)
            wave = []
            for plane in range(2):
                full = jnp.concatenate([back[plane * rows : (plane + 1) * rows], pad], 0)
                wave.append(dot(basis[...], full))
                if step == steps - 1:
                    out_ref[p, plane] = wave[plane].astype(bf16)
                yield

    filler = phases()
    chains = [chain(p) for p in range(probes)]
    live = list(range(probes))
    count = parts = 0
    while live:
        for p in list(live):
            if count < p * LAG:
                continue
            mark = next(chains[p], "end")
            if mark == "end":
                live.remove(p)
            elif mark is not None:
                while (mark, p) not in done:
                    next(filler)
            parts += 1
            if parts % PERIOD == 0:
                next(filler, None)
        count += 1
    for copy in sends.values():
        copy.wait_send()


def solution(mesh):
    n_lat, n_slc = mesh.shape["lat"], mesh.shape["slc"]
    window = 256

    def shards(atom_xy, atom_species, atom_slab, species_amp, species_spread, margin, probe_pos):
        square, prop = tables(window)
        atoms = atom_xy.shape[-1]
        field = float(n_lat * atoms * 4)
        probes = probe_pos.shape[0]
        vmem = pl.BlockSpec(memory_space=pltpu.VMEM)
        hbm = pl.BlockSpec(memory_space=pltpu.HBM)
        rows = prop.shape[1]
        layers = 2
        out = pl.pallas_call(
            functools.partial(kernel, n_lat, n_slc, window, field),
            out_shape=pltpu.VMEM((probes, 2, window, window), jnp.bfloat16),
            in_specs=[hbm] * 8,
            out_specs=vmem,
            scratch_shapes=[
                pltpu.SMEM(species_amp.shape, jnp.float32),
                pltpu.SMEM(species_spread.shape, jnp.float32),
                pltpu.SMEM(probe_pos.shape, jnp.int32),
                pltpu.VMEM(square.shape, jnp.bfloat16),
                pltpu.VMEM(prop.shape, jnp.float32),
                pltpu.VMEM((n_slc, 2, 2, LANES), jnp.float32),
                pltpu.VMEM((n_slc, 2, 2 * LANES), jnp.float32),
                pltpu.VMEM((n_slc, 2, 2, 1, LANES), jnp.int32),
                pltpu.VMEM((n_slc, 2, 1, 2 * LANES), jnp.int32),
                pltpu.VMEM((window, LANES), jnp.bfloat16),
                pltpu.VMEM((layers, probes, window, LANES), jnp.bfloat16),
                pltpu.VMEM((n_slc * layers, probes, 2, window, window), jnp.float32),
                pltpu.VMEM((probes, 2, window, window), jnp.bfloat16),
                pltpu.VMEM((probes, 2 * rows, window), jnp.bfloat16),
                pltpu.VMEM((probes, 2 * rows, window), jnp.bfloat16),
                pltpu.SemaphoreType.DMA((8,)),
                pltpu.SemaphoreType.DMA((n_slc, 3, 3)),
                pltpu.SemaphoreType.DMA((n_slc, 3, 3)),
            ],
            compiler_params=pltpu.CompilerParams(
                collective_id=0, has_side_effects=True, vmem_limit_bytes=int(63.4 * 2**20)
            ),
            name="multislice",
        )(atom_xy, atom_species, atom_slab, species_amp, species_spread, probe_pos,
          jnp.asarray(square), jnp.asarray(prop))
        return jnp.transpose(out, (0, 2, 1, 3))

    in_specs = (
        P(("groups", "lat"), "slc", None, None),
        P(("groups", "lat"), "slc", None),
        P(("groups", "lat"), "slc", None),
        P(),
        P(),
        P(("groups", "lat"), "slc", None, "rep", None, None),
        P(("groups", "lat", "slc", "rep"), None),
    )
    out_specs = P(("groups", "lat", "slc", "rep"), None, None, None)
    return jax.shard_map(shards, mesh=mesh, in_specs=in_specs, out_specs=out_specs, check_vma=False)
```
